32 devices in a mesh: groups: 2 (over x), dp: 16 (over z, y, core).
Axes of the slice: x: 2, y: 2, z: 4, core: 2. Of those that a mesh axis runs over, the one named last changes fastest.
Arguments:
- query: bfloat16 [16384, 4096], P(('groups', 'dp')), parts along dimension 0, may hold values from -6 to 6
- resp_key: bfloat16 [16384, 1024], P(('groups', 'dp')), parts along dimension 0, may hold values from -6 to 6
- resp_value: bfloat16 [16384, 1024], P(('groups', 'dp')), parts along dimension 0, may hold values from -6 to 6
- prompt_key: bfloat16 [2048, 1024], P(('groups', 'dp')), parts along dimension 0, may hold values from -6 to 6
- prompt_value: bfloat16 [2048, 1024], P(('groups', 'dp')), parts along dimension 0, may hold values from -6 to 6
- grad_out: bfloat16 [16384, 4096], P(('groups', 'dp')), parts along dimension 0, may hold values from -6 to 6
- resp_lengths: int32 [32, 4], P(('groups', 'dp')), parts along dimension 0, may hold values from 1 to 256, 512 in all within a row
- resp_prompt: int32 [32], P(('groups', 'dp')), parts along dimension 0, may hold values from 0 to 3
Outputs:
- grad_query: bfloat16 [16384, 4096], P(('groups', 'dp')), parts along dimension 0
- grad_resp_key: bfloat16 [16384, 1024], P(('groups', 'dp')), parts along dimension 0
- grad_resp_value: bfloat16 [16384, 1024], P(('groups', 'dp')), parts along dimension 0
- grad_prompt_key: bfloat16 [2048, 1024], P(('groups', 'dp')), parts along dimension 0
- grad_prompt_value: bfloat16 [2048, 1024], P(('groups', 'dp')), parts along dimension 0
The draws below stay inside these ranges and needn't reach their ends.
There are 2 independent parts, one for each index of `groups`. The reference program is written for one: setup_inputs(seed, part) draws one part's arguments, and reference() takes and returns one part's arrays. A program takes and returns all parts, laid end to end along the dimension named above; each array names one. Nothing has to cross between parts.
Inputs may be any that keep to these rules, and one draw needn't show every extreme that they name: `resp_lengths`: each row sums to 512.
All inputs are finite; a program needn't handle non-finite values.
Results may differ from the reference program's by a relative error of at most 0.0092.
Values may be sent and summed in bfloat16 or wider, within the bound.
A program may use at most 128 MiB of HBM per device.

```python
import math
import jax
import jax.numpy as jnp
import numpy as np
from jax import lax

HEADS = 32
KV_HEADS = 8
D_HEAD = 128
RT_DEV = 512
RESP_DEV = 4
PROMPTS = 4
PL = 256
RESP_ROWS = 8192
PROMPT_ROWS = 1024
N_DP = 16


def draw_query(key, part):
    own_key = jax.random.fold_in(key, 5)
    values = jax.random.normal(own_key, (RESP_ROWS, HEADS * D_HEAD), jnp.float32)
    return jnp.clip(values, -6.0, 6.0).astype(jnp.bfloat16)


def draw_prompt_key(key, part):
    own_key = jax.random.fold_in(key, 9)
    values = jax.random.normal(own_key, (PROMPT_ROWS, KV_HEADS * D_HEAD), jnp.float32)
    return jnp.clip(values, -6.0, 6.0).astype(jnp.bfloat16)


def with_ends(values, key, low, top_value):
    spot = [jax.random.randint(jax.random.fold_in(key, axis), (), 0, length) for axis, length in enumerate(values.shape)]
    longest = values.shape.index(max(values.shape))
    beside = spot[:longest] + [(spot[longest] + 1) % values.shape[longest]] + spot[longest + 1:]
    return values.at[tuple(spot)].set(low).at[tuple(beside)].set(top_value)


def level_of(key, extent, pieces, low, top_value):
    def one(dim, blocks):
        draws = jax.random.uniform(jax.random.fold_in(jax.random.fold_in(key, 6), dim), (blocks,), jnp.float32, low / len(pieces), top_value / len(pieces))
        return jnp.repeat(jnp.exp(draws), extent[dim] // blocks).reshape((-1,) + (1,) * (len(extent) - dim - 1))

    factor_of = one(*pieces[0])
    for cut in pieces[1:]:
        factor_of = factor_of * one(*cut)
    return factor_of


def profile(number_of, total, most, lean):
    loads = [(1 << 20) // math.isqrt(standing ** lean) + 1 for standing in range(2, number_of + 1)]
    rest, holding = total - most - (number_of - 1), [1] * (number_of - 1)
    while rest > 0:
        movable = [i for i in range(number_of - 1) if holding[i] < most]
        whole, budget = sum([loads[i] for i in movable]), rest
        for i in movable:
            addition = min(most - holding[i], max(1, budget * loads[i] // whole), rest)
            holding[i] = holding[i] + addition
            rest = rest - addition
    return np.array([most] + holding)


def ragged(key, amount, total, most, skew):
    if amount == 2:
        one = jax.random.randint(key, (), max(1, total - most), min(most, total - 1) + 1)
        return jnp.stack([one, total - one])
    sizes = jnp.asarray(profile(amount, total, most, skew), jnp.int32)
    couples = (amount - 1) // 2
    donor, sink = sizes[1:1 + 2 * couples:2], sizes[2:2 + 2 * couples:2]
    room = jnp.minimum(donor - 1, most - sink)
    shifted = jax.random.randint(jax.random.fold_in(key, 1), (couples,), 0, 1 << 20) % (room + 1)
    sizes = sizes.at[1:1 + 2 * couples:2].set(donor - shifted).at[2:2 + 2 * couples:2].set(sink + shifted)
    return sizes[jax.random.permutation(jax.random.fold_in(key, 2), amount)]


def centred(key, extent, scale, reach, shards=(), kind=jnp.bfloat16):
    values = scale * jax.random.normal(key, extent, jnp.float32)
    if shards:
        values = values * level_of(key, extent, shards, -0.22, 0.18)
    return jnp.clip(values, -reach, reach).astype(kind)


def setup_inputs(seed: int = 0, part: int = 0) -> dict:
    seeds = jax.random.split(jax.random.key(seed), 9)
    part_keys = jax.random.split(jax.random.fold_in(seeds[8], part), 9)
    return {
        "query": draw_query(jax.random.fold_in(jax.random.fold_in(seeds[8], part), 71), part),
        "resp_key": centred(part_keys[1], (RESP_ROWS, KV_HEADS * D_HEAD), 1.0, 6.0, ((0, 16),)),
        "resp_value": centred(part_keys[2], (RESP_ROWS, KV_HEADS * D_HEAD), 1.0, 6.0, ((0, 16),)),
        "prompt_key": draw_prompt_key(jax.random.fold_in(jax.random.fold_in(seeds[8], part), 71), part),
        "prompt_value": centred(part_keys[4], (PROMPT_ROWS, KV_HEADS * D_HEAD), 1.0, 6.0, ((0, 16),)),
        "grad_out": centred(part_keys[5], (RESP_ROWS, HEADS * D_HEAD), 1.0, 6.0, ((0, 16),)),
        "resp_lengths": jax.vmap(lambda own: ragged(own, RESP_DEV, RT_DEV, RT_DEV // 2, 2))(jax.random.split(part_keys[6], N_DP)).reshape((N_DP, RESP_DEV)).astype(jnp.int32),
        "resp_prompt": with_ends(jax.random.randint(part_keys[7], (N_DP,), 0, PROMPTS), jax.random.fold_in(part_keys[7], 1), 0, PROMPTS - 1).astype(jnp.int32),
    }


def allowed_mask(lengths, prompt_rows, rows):
    ends = jnp.cumsum(lengths)
    place = jnp.arange(rows, dtype=jnp.int32)
    segment = jnp.sum((place[:, None] >= ends[None, :]).astype(jnp.int32), axis=1)
    own = (segment[:, None] == segment[None, :]) & (place[None, :] <= place[:, None])
    return jnp.concatenate([jnp.ones((rows, prompt_rows), bool), own], axis=1)


def head_step(mask, q_head, k_head, v_head, g_head):
    scale = D_HEAD ** -0.5
    qf = q_head.astype(jnp.float32)
    kf = k_head.astype(jnp.float32)
    vf = v_head.astype(jnp.float32)
    gf = g_head.astype(jnp.float32)
    scores = jnp.einsum("qgd,sd->gqs", qf, kf) * scale
    scores = jnp.where(mask[None], scores, -1e30)
    top = jnp.max(scores, axis=-1, keepdims=True)
    expo = jnp.exp(scores - top)
    probs = expo / jnp.sum(expo, axis=-1, keepdims=True)
    weights = probs.astype(jnp.bfloat16)
    wf = weights.astype(jnp.float32)
    out = jnp.einsum("gqs,sd->qgd", wf, vf)
    dprob = jnp.einsum("qgd,sd->gqs", gf, vf)
    delta = jnp.sum(gf * out, axis=-1).transpose(1, 0)[:, :, None]
    dscore = (probs * (dprob - delta) * scale).astype(jnp.bfloat16)
    df = dscore.astype(jnp.float32)
    grad_q = jnp.einsum("gqs,sd->qgd", df, kf).astype(jnp.bfloat16)
    grad_k = jnp.einsum("gqs,qgd->sd", df, qf)
    grad_v = jnp.einsum("gqs,qgd->sd", wf, gf)
    return grad_q, grad_k, grad_v


def reference(query, resp_key, resp_value, prompt_key, prompt_value, grad_out, resp_lengths, resp_prompt):
    group = HEADS // KV_HEADS
    width = KV_HEADS * D_HEAD
    query_b = query.reshape(N_DP, RT_DEV, KV_HEADS, group, D_HEAD)
    grad_b = grad_out.reshape(N_DP, RT_DEV, KV_HEADS, group, D_HEAD)
    key_b = resp_key.reshape(N_DP, RT_DEV, width)
    value_b = resp_value.reshape(N_DP, RT_DEV, width)

    def one_block(totals, inputs):
        q_blk, g_blk, k_blk, v_blk, lengths, prompt_id = inputs
        start = (prompt_id * PL).astype(jnp.int32)
        pk = lax.dynamic_slice_in_dim(prompt_key, start, PL, 0)
        pv = lax.dynamic_slice_in_dim(prompt_value, start, PL, 0)
        keys = jnp.concatenate([pk, k_blk], 0).reshape(-1, KV_HEADS, D_HEAD).transpose(1, 0, 2)
        values = jnp.concatenate([pv, v_blk], 0).reshape(-1, KV_HEADS, D_HEAD).transpose(1, 0, 2)
        mask = allowed_mask(lengths, PL, RT_DEV)
        grad_q, grad_k, grad_v = lax.map(lambda xs: head_step(mask, *xs), (q_blk.transpose(1, 0, 2, 3), keys, values, g_blk.transpose(1, 0, 2, 3)))
        grad_q = grad_q.transpose(1, 0, 2, 3).reshape(RT_DEV, HEADS * D_HEAD)
        grad_k = grad_k.transpose(1, 0, 2).reshape(-1, width)
        grad_v = grad_v.transpose(1, 0, 2).reshape(-1, width)
        total_k, total_v = totals
        total_k = lax.dynamic_update_slice_in_dim(total_k, lax.dynamic_slice_in_dim(total_k, start, PL, 0) + grad_k[:PL], start, 0)
        total_v = lax.dynamic_update_slice_in_dim(total_v, lax.dynamic_slice_in_dim(total_v, start, PL, 0) + grad_v[:PL], start, 0)
        return (total_k, total_v), (grad_q, grad_k[PL:].astype(jnp.bfloat16), grad_v[PL:].astype(jnp.bfloat16))

    zero = jnp.zeros((PROMPT_ROWS, width), jnp.float32)
    (total_k, total_v), (grad_q, grad_rk, grad_rv) = lax.scan(one_block, (zero, zero), (query_b, grad_b, key_b, value_b, resp_lengths, resp_prompt))
    return (grad_q.reshape(RESP_ROWS, HEADS * D_HEAD), grad_rk.reshape(RESP_ROWS, width), grad_rv.reshape(RESP_ROWS, width), total_k.astype(jnp.bfloat16), total_v.astype(jnp.bfloat16))
```

```python
import functools

import jax
import jax.numpy as jnp
from jax import lax
from jax.experimental import pallas as pl
from jax.experimental.pallas import tpu as pltpu
from jax.sharding import PartitionSpec as P

HEADS = 32
KV_HEADS = 8
D_HEAD = 128
GROUP = HEADS // KV_HEADS
RESP_MAX = 256
QB = 128
SCALE = D_HEAD ** (-0.5)
LOG2E = 1.4426950408889634
F32 = jnp.float32
BF16 = jnp.bfloat16


def dot(a, b, ca, cb):
    return lax.dot_general(a, b, (((ca,), (cb,)), ((), ())), preferred_element_type=F32)


def fill_bias(lens, bias_ref):
    rows = bias_ref.shape[0]
    place = lax.broadcasted_iota(jnp.int32, (1, rows), 1)
    begin = jnp.zeros((1, rows), jnp.int32)
    end = jnp.int32(0)
    for i in range(len(lens)):
        end = end + lens[i]
        begin = jnp.where(place >= end, end, begin)
    key = lax.broadcasted_iota(jnp.int32, (rows, rows), 0)
    ok = (key >= begin) & (key <= place)
    bias_ref[...] = jnp.where(ok, 0.0, -1e30)


def head_grads(q_ref, g_ref, pk, pv, rk_ref, rv_ref, bias_ref, gq_ref, acc_k, acc_v, lane0):
    rows = bias_ref.shape[0]
    plen = pk.shape[0]
    back = -(-(RESP_MAX - 1) // QB) * QB
    acc_k[...] = jnp.zeros_like(acc_k)
    acc_v[...] = jnp.zeros_like(acc_v)
    for q0 in range(0, rows, QB):
        lo, hi = max(0, q0 - back), q0 + QB

        def stacked(ref):
            return jnp.concatenate(
                [ref[q0:hi, j * D_HEAD:(j + 1) * D_HEAD] for j in range(GROUP)], 0
            )

        q, g = stacked(q_ref), stacked(g_ref)
        k = jnp.concatenate([pk, rk_ref[lo:hi, :]], 0)
        v = jnp.concatenate([pv, rv_ref[lo:hi, :]], 0)
        s = dot(k, q, 1, 1)
        bias = bias_ref[lo:hi, q0:hi]
        s_p = s[:plen]
        s_r = s[plen:] + jnp.concatenate([bias] * GROUP, 1)
        top = jnp.maximum(
            jnp.max(s_p, axis=0, keepdims=True), jnp.max(s_r, axis=0, keepdims=True)
        )
        e = jnp.concatenate([s_p, s_r], 0) - top
        e = jnp.exp2(e * (SCALE * LOG2E))
        inv = 1.0 / jnp.sum(e, axis=0, keepdims=True)
        dp = dot(v, g, 1, 1)
        delta = jnp.sum(e * dp, axis=0, keepdims=True) * inv
        p = e * inv
        w = p.astype(BF16)
        ds = (p * (dp - delta)).astype(BF16)
        gv = dot(w, g, 1, 0)
        gk = dot(ds, q, 1, 0)
        acc_v[:plen, :] += gv[:plen]
        acc_v[plen + lo:plen + hi, :] += gv[plen:]
        acc_k[:plen, :] += gk[:plen]
        acc_k[plen + lo:plen + hi, :] += gk[plen:]
        gq = dot(k, ds, 0, 0) * SCALE
        for j in range(GROUP):
            gq_ref[q0:hi, j * D_HEAD:(j + 1) * D_HEAD] = (
                gq[:, j * QB:(j + 1) * QB].T.astype(BF16)
            )


def kernel(which, lens_ref, q_ref, g_ref, pk_ref, pv_ref, rk_ref, rv_ref,
           gq_ref, grk_ref, grv_ref, gpk_ref, gpv_ref, bias_ref, acc_k, acc_v):
    @pl.when(pl.program_id(0) == 0)
    def _():
        fill_bias([lens_ref[0, i] for i in range(lens_ref.shape[1])], bias_ref)

    plen = pk_ref.shape[0]
    head_grads(q_ref, g_ref, pk_ref[...], pv_ref[...], rk_ref, rv_ref, bias_ref, gq_ref,
               acc_k, acc_v, 0)
    gpk_ref[...] = (acc_k[:plen, :] * SCALE).astype(BF16)
    gpv_ref[...] = acc_v[:plen, :].astype(BF16)
    grk_ref[...] = (acc_k[plen:, :] * SCALE).astype(BF16)
    grv_ref[...] = acc_v[plen:, :].astype(BF16)


def attention(which, lengths, query, grad_out, keys, resp_key, resp_value, plen):
    rows = query.shape[0]
    width = KV_HEADS * D_HEAD
    wide = pl.BlockSpec((rows, GROUP * D_HEAD), lambda h, w: (0, h))
    own = pl.BlockSpec((rows, D_HEAD), lambda h, w: (0, h))
    out_p = pl.BlockSpec((plen, D_HEAD), lambda h, w: (0, h))
    sds = jax.ShapeDtypeStruct
    return pl.pallas_call(
        kernel,
        grid_spec=pltpu.PrefetchScalarGridSpec(
            num_scalar_prefetch=1,
            grid=(KV_HEADS,),
            in_specs=[
                pl.BlockSpec(memory_space=pltpu.SMEM),
                wide,
                wide,
                pl.BlockSpec((plen, D_HEAD), lambda h, w: (w[0], h)),
                pl.BlockSpec((plen, D_HEAD), lambda h, w: (w[0], h + KV_HEADS)),
                own,
                own,
            ],
            out_specs=[wide, own, own, out_p, out_p],
            scratch_shapes=[
                pltpu.VMEM((rows, rows), F32),
                pltpu.VMEM((plen + rows, D_HEAD), F32),
                pltpu.VMEM((plen + rows, D_HEAD), F32),
            ],
        ),
        out_shape=[
            sds((rows, HEADS * D_HEAD), BF16),
            sds((rows, width), BF16),
            sds((rows, width), BF16),
            sds((plen, width), BF16),
            sds((plen, width), BF16),
        ],
        compiler_params=pltpu.CompilerParams(
            dimension_semantics=("arbitrary",), vmem_limit_bytes=40 * 1024 * 1024
        ),
    )(which, lengths, query, grad_out, keys, keys, resp_key, resp_value)


def shards(
    query, resp_key, resp_value, prompt_key, prompt_value, grad_out, resp_lengths, resp_prompt
):
    own_rows = prompt_key.shape[0]
    plen = 4 * own_rows
    width = KV_HEADS * D_HEAD
    every = lax.all_gather(
        jnp.concatenate([prompt_key, prompt_value], 1), "dp", axis=0, tiled=True
    )
    gq, grk, grv, gpk, gpv = attention(
        resp_prompt, resp_lengths, query, grad_out, every, resp_key, resp_value, plen
    )
    terms = jnp.zeros((own_rows * lax.axis_size("dp"), 2 * width), BF16)
    terms = lax.dynamic_update_slice(
        terms, jnp.concatenate([gpk, gpv], 1), (resp_prompt[0] * plen, 0)
    )
    summed = lax.psum_scatter(terms, "dp", scatter_dimension=0, tiled=True)
    return gq, grk, grv, summed[:, :width], summed[:, width:]


def solution(mesh):
    rows = P(("groups", "dp"), None)
    return jax.shard_map(
        shards,
        mesh=mesh,
        in_specs=(rows,) * 7 + (P(("groups", "dp")),),
        out_specs=(rows,) * 5,
        check_vma=False,
    )
```

```python
import jax
import jax.numpy as jnp
from jax import lax
from jax.experimental import pallas as pl
from jax.experimental.pallas import tpu as pltpu
from jax.sharding import PartitionSpec as P

HEADS = 32
KV_HEADS = 8
D_HEAD = 128
GROUP = HEADS // KV_HEADS
RESP_MAX = 256
QB = 128
SCALE = D_HEAD ** (-0.5)
LOG2E = 1.4426950408889634
F32 = jnp.float32
BF16 = jnp.bfloat16


def dot(a, b, ca, cb):
    return lax.dot_general(a, b, (((ca,), (cb,)), ((), ())), preferred_element_type=F32)


def fill_bias(lens, bias_ref):
    rows = bias_ref.shape[0]
    place = lax.broadcasted_iota(jnp.int32, (1, rows), 1)
    begin = jnp.zeros((1, rows), jnp.int32)
    end = jnp.int32(0)
    for i in range(len(lens)):
        end = end + lens[i]
        begin = jnp.where(place >= end, end, begin)
    key = lax.broadcasted_iota(jnp.int32, (rows, rows), 0)
    ok = (key >= begin) & (key <= place)
    bias_ref[...] = jnp.where(ok, 0.0, -1e30)


def head_grads(q_ref, g_ref, pk, pv, rk_ref, rv_ref, bias_ref, gq_ref, acc_k, acc_v, lane0):
    rows = bias_ref.shape[0]
    plen = pk.shape[0]
    back = -(-(RESP_MAX - 1) // QB) * QB
    acc_k[...] = jnp.zeros_like(acc_k)
    acc_v[...] = jnp.zeros_like(acc_v)
    for q0 in range(0, rows, QB):
        lo, hi = max(0, q0 - back), q0 + QB

        def stacked(ref):
            return jnp.concatenate(
                [ref[q0:hi, j * D_HEAD:(j + 1) * D_HEAD] for j in range(GROUP)], 0
            )

        q, g = stacked(q_ref), stacked(g_ref)
        k = jnp.concatenate([pk, rk_ref[lo:hi, :]], 0)
        v = jnp.concatenate([pv, rv_ref[lo:hi, :]], 0)
        s = dot(k, q, 1, 1)
        bias = bias_ref[lo:hi, q0:hi]
        s_p = s[:plen]
        s_r = s[plen:] + jnp.concatenate([bias] * GROUP, 1)
        top = jnp.maximum(
            jnp.max(s_p, axis=0, keepdims=True), jnp.max(s_r, axis=0, keepdims=True)
        )
        e = jnp.concatenate([s_p, s_r], 0) - top
        e = jnp.exp2(e * (SCALE * LOG2E))
        inv = 1.0 / jnp.sum(e, axis=0, keepdims=True)
        dp = dot(v, g, 1, 1)
        delta = jnp.sum(e * dp, axis=0, keepdims=True) * inv
        p = e * inv
        w = p.astype(BF16)
        ds = (p * (dp - delta)).astype(BF16)
        gv = dot(w, g, 1, 0)
        gk = dot(ds, q, 1, 0)
        acc_v[:plen, :] += gv[:plen]
        acc_v[plen + lo:plen + hi, :] += gv[plen:]
        acc_k[:plen, :] += gk[:plen]
        acc_k[plen + lo:plen + hi, :] += gk[plen:]
        gq = dot(k, ds, 0, 0) * SCALE
        for j in range(GROUP):
            gq_ref[q0:hi, j * D_HEAD:(j + 1) * D_HEAD] = (
                gq[:, j * QB:(j + 1) * QB].T.astype(BF16)
            )


QUARTERS = 4
MESH = pl.DeviceIdType.MESH


def kernel(which_ref, lens_ref, q_ref, g_ref, pk_ref, pv_ref, rk_ref, rv_ref,
           gq_ref, grk_ref, grv_ref, gpk_ref, gpv_ref,
           bias_ref, acc_k, acc_v, buf, cbuf, dbuf, ebuf, fbuf, ids,
           a_send, a_recv, b_send, b_recv, c_send, c_recv, d_send, d_recv,
           e_send, e_recv, i_send, i_recv):
    t = pl.program_id(0)
    planes = buf.shape[3]
    own_rows = pk_ref.shape[0]
    plen = QUARTERS * own_rows
    me = lax.axis_index("dp")
    lo, hi = me % QUARTERS, me // QUARTERS
    core, row = lo % 2, lo // 2
    other_core = me + 1 - 2 * core
    other_row = me + 2 - 4 * row

    def to(src, dst, send, recv, dev):
        return pltpu.make_async_remote_copy(
            src_ref=src, dst_ref=dst, send_sem=send, recv_sem=recv,
            device_id={"dp": dev}, device_id_type=MESH,
        )

    def planes_of(h, j):
        mine = buf.at[h, row, core, hi]
        return to(mine, mine, a_send.at[h, j - 1], a_recv.at[h, j - 1],
                  (hi + j) % planes * QUARTERS + lo)

    def rows_of(h):
        part = buf.at[h, row, core]
        return to(part, part, b_send.at[h], b_recv.at[h], other_row)

    def cores_of(h, r):
        part = buf.at[h, r, core]
        return to(part, part, c_send.at[h, r], c_recv.at[h, r], other_core)

    def quarter_to(h, j):
        peer = (lo + j) % QUARTERS
        return to(cbuf.at[h, peer], dbuf.at[h, lo], d_send.at[h, j - 1], d_recv.at[h, j - 1],
                  hi * QUARTERS + peer)

    def id_to(j):
        return to(ids.at[lo], ids.at[lo], i_send.at[j - 1], i_recv.at[j - 1],
                  hi * QUARTERS + (lo + j) % QUARTERS)

    def term_to(h, j):
        peer = (hi + j) % planes
        return to(ebuf.at[h, peer], fbuf.at[h, hi], e_send.at[h, j - 1], e_recv.at[h, j - 1],
                  peer * QUARTERS + lo)

    def start_rows(h):
        for j in range(1, planes):
            planes_of(h, j).wait_recv()
        rows_of(h).start()

    def start_cores(h):
        rows_of(h).wait_recv()
        for r in range(2):
            cores_of(h, r).start()

    def reduce_group(h):
        for j in range(1, QUARTERS):
            quarter_to(h, j).wait_recv()
        for p in range(planes):
            total = None
            for i in range(QUARTERS):
                flag = jnp.where(ids[i, 0:1, :] == float(p), 1.0, 0.0)
                flag = jnp.concatenate([flag, flag], 1)
                term = dbuf[h, i].astype(F32) * flag
                total = term if total is None else total + term
            ebuf[h, p] = total.astype(BF16)
        fbuf[h, hi] = ebuf[h, hi]
        for j in range(1, planes):
            term_to(h, j).start()

    def reduce_planes(h):
        for j in range(1, planes):
            term_to(h, j).wait_recv()
        total = fbuf[h, 0].astype(F32)
        for p in range(1, planes):
            total = total + fbuf[h, p].astype(F32)
        cols = pl.ds(pl.multiple_of(h * D_HEAD, D_HEAD), D_HEAD)
        gpk_ref[:, cols] = total[:, :D_HEAD].astype(BF16)
        gpv_ref[:, cols] = total[:, D_HEAD:].astype(BF16)

    @pl.when(t == 0)
    def _():
        barrier = pltpu.get_barrier_semaphore()
        for j in range(1, planes):
            pl.semaphore_signal(barrier, inc=1, device_id_type=MESH,
                                device_id={"dp": (hi + j) % planes * QUARTERS + lo})
        for j in range(1, QUARTERS):
            pl.semaphore_signal(barrier, inc=1, device_id_type=MESH,
                                device_id={"dp": hi * QUARTERS + (lo + j) % QUARTERS})
        for h in range(KV_HEADS):
            cols = slice(h * D_HEAD, (h + 1) * D_HEAD)
            buf[h, row, core, hi] = jnp.concatenate([pk_ref[:, cols], pv_ref[:, cols]], 1)
        ids[lo] = jnp.full(ids.shape[1:], which_ref[0], jnp.int32).astype(F32)
        pl.semaphore_wait(barrier, planes - 1 + QUARTERS - 1)

        @pl.loop(0, KV_HEADS)
        def _(h):
            for j in range(1, planes):
                planes_of(h, j).start()

        for j in range(1, QUARTERS):
            id_to(j).start()
        fill_bias([lens_ref[0, i] for i in range(lens_ref.shape[1])], bias_ref)
        start_rows(0)
        start_rows(1)
        start_cores(0)
        for j in range(1, QUARTERS):
            id_to(j).wait()

    @pl.when(t + 2 < KV_HEADS)
    def _():
        start_rows(t + 2)

    @pl.when(t + 1 < KV_HEADS)
    def _():
        start_cores(t + 1)

    for r in range(2):
        cores_of(t, r).wait_recv()
    parts = []
    for i in range(QUARTERS):
        picked = None
        for p in range(planes):
            flag = jnp.where(ids[lo, 0:1, :] == float(p), 1.0, 0.0)
            flag = jnp.concatenate([flag, flag], 1)
            term = buf[t, i // 2, i % 2, p].astype(F32) * flag
            picked = term if picked is None else picked + term
        parts.append(picked.astype(BF16))
    prompt = jnp.concatenate(parts, 0)

    head_grads(q_ref, g_ref, prompt[:, :D_HEAD], prompt[:, D_HEAD:], rk_ref, rv_ref, bias_ref,
               gq_ref, acc_k, acc_v, 0)
    for i in range(QUARTERS):
        rows = slice(i * own_rows, (i + 1) * own_rows)
        cbuf[t, i] = jnp.concatenate([acc_k[rows, :] * SCALE, acc_v[rows, :]], 1).astype(BF16)
    dbuf[t, lo] = cbuf[t, lo]
    for j in range(1, QUARTERS):
        quarter_to(t, j).start()
    grk_ref[...] = (acc_k[plen:, :] * SCALE).astype(BF16)
    grv_ref[...] = acc_v[plen:, :].astype(BF16)

    @pl.when(t >= 1)
    def _():
        reduce_group(t - 1)

    @pl.when(t >= 2)
    def _():
        reduce_planes(t - 2)

    @pl.when(t == KV_HEADS - 1)
    def _():
        reduce_group(KV_HEADS - 1)
        reduce_planes(KV_HEADS - 2)
        reduce_planes(KV_HEADS - 1)

        @pl.loop(0, KV_HEADS)
        def _(h):
            for j in range(1, planes):
                planes_of(h, j).wait_send()
                term_to(h, j).wait_send()
            rows_of(h).wait_send()
            for r in range(2):
                cores_of(h, r).wait_send()
            for j in range(1, QUARTERS):
                quarter_to(h, j).wait_send()


def shards(
    query, resp_key, resp_value, prompt_key, prompt_value, grad_out, resp_lengths, resp_prompt
):
    rows = query.shape[0]
    own_rows = prompt_key.shape[0]
    plen = QUARTERS * own_rows
    width = KV_HEADS * D_HEAD
    planes = lax.axis_size("dp") // QUARTERS
    wide = pl.BlockSpec((rows, GROUP * D_HEAD), lambda h: (0, h))
    own = pl.BlockSpec((rows, D_HEAD), lambda h: (0, h))
    whole = pl.BlockSpec((own_rows, width), lambda h: (0, 0))
    smem = pl.BlockSpec(memory_space=pltpu.SMEM)
    sds = jax.ShapeDtypeStruct
    pair = (own_rows, 2 * D_HEAD)
    dma = pltpu.SemaphoreType.DMA
    return pl.pallas_call(
        kernel,
        grid=(KV_HEADS,),
        in_specs=[smem, smem, wide, wide, whole, whole, own, own],
        out_specs=[wide, own, own, whole, whole],
        scratch_shapes=[
            pltpu.VMEM((rows, rows), F32),
            pltpu.VMEM((plen + rows, D_HEAD), F32),
            pltpu.VMEM((plen + rows, D_HEAD), F32),
            pltpu.VMEM((KV_HEADS, 2, 2, planes) + pair, BF16),
            pltpu.VMEM((KV_HEADS, QUARTERS) + pair, BF16),
            pltpu.VMEM((KV_HEADS, QUARTERS) + pair, BF16),
            pltpu.VMEM((KV_HEADS, planes) + pair, BF16),
            pltpu.VMEM((KV_HEADS, planes) + pair, BF16),
            pltpu.VMEM((QUARTERS, 8, 128), F32),
            dma((KV_HEADS, planes - 1)),
            dma((KV_HEADS, planes - 1)),
            dma((KV_HEADS,)),
            dma((KV_HEADS,)),
            dma((KV_HEADS, 2)),
            dma((KV_HEADS, 2)),
            dma((KV_HEADS, QUARTERS - 1)),
            dma((KV_HEADS, QUARTERS - 1)),
            dma((KV_HEADS, planes - 1)),
            dma((KV_HEADS, planes - 1)),
            dma((QUARTERS - 1,)),
            dma((QUARTERS - 1,)),
        ],
        out_shape=[
            sds((rows, HEADS * D_HEAD), BF16),
            sds((rows, width), BF16),
            sds((rows, width), BF16),
            sds((own_rows, width), BF16),
            sds((own_rows, width), BF16),
        ],
        compiler_params=pltpu.CompilerParams(
            dimension_semantics=("arbitrary",), vmem_limit_bytes=48 * 1024 * 1024,
            collective_id=0, has_side_effects=True,
        ),
    )(resp_prompt, resp_lengths, query, grad_out, prompt_key, prompt_value, resp_key, resp_value)


def solution(mesh):
    rows = P(("groups", "dp"), None)
    return jax.shard_map(
        shards,
        mesh=mesh,
        in_specs=(rows,) * 7 + (P(("groups", "dp")),),
        out_specs=(rows,) * 5,
        check_vma=False,
    )
```

```python
import jax
import jax.numpy as jnp
from jax import lax
from jax.experimental import pallas as pl
from jax.experimental.pallas import tpu as pltpu
from jax.sharding import PartitionSpec as P

HEADS = 32
KV_HEADS = 8
D_HEAD = 128
GROUP = HEADS // KV_HEADS
RESP_MAX = 256
QB = 128
SCALE = D_HEAD ** (-0.5)
LOG2E = 1.4426950408889634
F32 = jnp.float32
BF16 = jnp.bfloat16


def dot(a, b, ca, cb):
    return lax.dot_general(a, b, (((ca,), (cb,)), ((), ())), preferred_element_type=F32)


def fill_bias(lens, bias_ref):
    rows = bias_ref.shape[0]
    place = lax.broadcasted_iota(jnp.int32, (1, rows), 1)
    begin = jnp.zeros((1, rows), jnp.int32)
    end = jnp.int32(0)
    for i in range(len(lens)):
        end = end + lens[i]
        begin = jnp.where(place >= end, end, begin)
    key = lax.broadcasted_iota(jnp.int32, (rows, rows), 0)
    ok = (key >= begin) & (key <= place)
    bias_ref[...] = jnp.where(ok, 0.0, -1e30)


def head_grads(q_ref, g_ref, pk, pv, rk_ref, rv_ref, bias_ref, gq_ref, acc_k, acc_v, lane0):
    rows = bias_ref.shape[0]
    plen = pk.shape[0]
    back = -(-(RESP_MAX - 1) // QB) * QB
    acc_k[...] = jnp.zeros_like(acc_k)
    acc_v[...] = jnp.zeros_like(acc_v)
    for q0 in range(0, rows, QB):
        lo, hi = max(0, q0 - back), q0 + QB

        def stacked(ref):
            return jnp.concatenate(
                [ref[q0:hi, j * D_HEAD:(j + 1) * D_HEAD] for j in range(GROUP)], 0
            )

        q, g = stacked(q_ref), stacked(g_ref)
        k = jnp.concatenate([pk, rk_ref[lo:hi, :]], 0)
        v = jnp.concatenate([pv, rv_ref[lo:hi, :]], 0)
        s = dot(k, q, 1, 1)
        bias = bias_ref[lo:hi, q0:hi]
        s_p = s[:plen]
        s_r = s[plen:] + jnp.concatenate([bias] * GROUP, 1)
        top = jnp.maximum(
            jnp.max(s_p, axis=0, keepdims=True), jnp.max(s_r, axis=0, keepdims=True)
        )
        e = jnp.concatenate([s_p, s_r], 0) - top
        e = jnp.exp2(e * (SCALE * LOG2E))
        inv = 1.0 / jnp.sum(e, axis=0, keepdims=True)
        dp = dot(v, g, 1, 1)
        delta = jnp.sum(e * dp, axis=0, keepdims=True) * inv
        p = e * inv
        w = p.astype(BF16)
        ds = (p * (dp - delta)).astype(BF16)
        gv = dot(w, g, 1, 0)
        gk = dot(ds, q, 1, 0)
        acc_v[:plen, :] += gv[:plen]
        acc_v[plen + lo:plen + hi, :] += gv[plen:]
        acc_k[:plen, :] += gk[:plen]
        acc_k[plen + lo:plen + hi, :] += gk[plen:]
        gq = dot(k, ds, 0, 0) * SCALE
        for j in range(GROUP):
            gq_ref[q0:hi, j * D_HEAD:(j + 1) * D_HEAD] = (
                gq[:, j * QB:(j + 1) * QB].T.astype(BF16)
            )


QUARTERS = 4
MESH = pl.DeviceIdType.MESH


def kernel(which_ref, lens_ref, q_ref, g_ref, pk_ref, pv_ref, rk_ref, rv_ref,
           gq_ref, grk_ref, grv_ref, gpk_ref, gpv_ref,
           bias_ref, acc_k, acc_v, buf, cbuf, dbuf, ebuf, fbuf, ids,
           a_send, a_recv, b_send, b_recv, c_send, c_recv, d_send, d_recv,
           e_send, e_recv, i_send, i_recv):
    t = pl.program_id(0)
    planes = buf.shape[3]
    own_rows = pk_ref.shape[0]
    plen = QUARTERS * own_rows
    me = lax.axis_index("dp")
    lo, hi = me % QUARTERS, me // QUARTERS
    core, row = lo % 2, lo // 2
    other_core = me + 1 - 2 * core
    other_row = me + 2 - 4 * row

    def to(src, dst, send, recv, dev):
        return pltpu.make_async_remote_copy(
            src_ref=src, dst_ref=dst, send_sem=send, recv_sem=recv,
            device_id={"dp": dev}, device_id_type=MESH,
        )

    def planes_of(h, j):
        mine = buf.at[h, row, core, hi]
        return to(mine, mine, a_send.at[h, j - 1], a_recv.at[h, j - 1],
                  (hi + j) % planes * QUARTERS + lo)

    def rows_of(h):
        part = buf.at[h, row, core]
        return to(part, part, b_send.at[h], b_recv.at[h], other_row)

    def cores_of(h, r):
        part = buf.at[h, r, core]
        return to(part, part, c_send.at[h, r], c_recv.at[h, r], other_core)

    def quarter_to(h, j):
        peer = (lo + j) % QUARTERS
        return to(cbuf.at[h, peer], dbuf.at[h, lo], d_send.at[h, j - 1], d_recv.at[h, j - 1],
                  hi * QUARTERS + peer)

    def id_to(j):
        return to(ids.at[lo], ids.at[lo], i_send.at[j - 1], i_recv.at[j - 1],
                  hi * QUARTERS + (lo + j) % QUARTERS)

    def term_to(h, j):
        peer = (hi + j) % planes
        return to(ebuf.at[h, peer], fbuf.at[h, hi], e_send.at[h, j - 1], e_recv.at[h, j - 1],
                  peer * QUARTERS + lo)

    def start_rows(h):
        for j in range(1, planes):
            planes_of(h, j).wait_recv()
        rows_of(h).start()

    def start_cores(h):
        rows_of(h).wait_recv()
        for r in range(2):
            cores_of(h, r).start()

    def reduce_group(h):
        for j in range(1, QUARTERS):
            quarter_to(h, j).wait_recv()
        for p in range(planes):
            total = None
            for i in range(QUARTERS):
                flag = jnp.where(ids[i, 0:1, :] == float(p), 1.0, 0.0)
                flag = jnp.concatenate([flag, flag], 1)
                term = dbuf[h, i].astype(F32) * flag
                total = term if total is None else total + term
            ebuf[h, p] = total.astype(BF16)
        fbuf[h, hi] = ebuf[h, hi]
        for j in range(1, planes):
            term_to(h, j).start()

    def reduce_planes(h):
        for j in range(1, planes):
            term_to(h, j).wait_recv()
        total = fbuf[h, 0].astype(F32)
        for p in range(1, planes):
            total = total + fbuf[h, p].astype(F32)
        cols = pl.ds(pl.multiple_of(h * D_HEAD, D_HEAD), D_HEAD)
        gpk_ref[:, cols] = total[:, :D_HEAD].astype(BF16)
        gpv_ref[:, cols] = total[:, D_HEAD:].astype(BF16)

    @pl.when(t == 0)
    def _():
        barrier = pltpu.get_barrier_semaphore()
        for j in range(1, planes):
            pl.semaphore_signal(barrier, inc=1, device_id_type=MESH,
                                device_id={"dp": (hi + j) % planes * QUARTERS + lo})
        for j in range(1, QUARTERS):
            pl.semaphore_signal(barrier, inc=1, device_id_type=MESH,
                                device_id={"dp": hi * QUARTERS + (lo + j) % QUARTERS})
        for h in range(KV_HEADS):
            cols = slice(h * D_HEAD, (h + 1) * D_HEAD)
            buf[h, row, core, hi] = jnp.concatenate([pk_ref[:, cols], pv_ref[:, cols]], 1)
        ids[lo] = jnp.full(ids.shape[1:], which_ref[0], jnp.int32).astype(F32)
        pl.semaphore_wait(barrier, planes - 1 + QUARTERS - 1)

        @pl.loop(0, KV_HEADS)
        def _(h):
            for j in range(1, planes):
                planes_of(h, j).start()

        for j in range(1, QUARTERS):
            id_to(j).start()
        fill_bias([lens_ref[0, i] for i in range(lens_ref.shape[1])], bias_ref)
        start_rows(0)
        start_rows(1)
        start_cores(0)
        for j in range(1, QUARTERS):
            id_to(j).wait()

    @pl.when(t + 2 < KV_HEADS)
    def _():
        start_rows(t + 2)

    @pl.when(t + 1 < KV_HEADS)
    def _():
        start_cores(t + 1)

    for r in range(2):
        cores_of(t, r).wait_recv()
    parts = []
    for i in range(QUARTERS):
        picked = None
        for p in range(planes):
            flag = jnp.where(ids[lo, 0:1, :] == float(p), 1.0, 0.0)
            flag = jnp.concatenate([flag, flag], 1)
            term = buf[t, i // 2, i % 2, p].astype(F32) * flag
            picked = term if picked is None else picked + term
        parts.append(picked.astype(BF16))
    prompt = jnp.concatenate(parts, 0)

    head_grads(q_ref, g_ref, prompt[:, :D_HEAD], prompt[:, D_HEAD:], rk_ref, rv_ref, bias_ref,
               gq_ref, acc_k, acc_v, 0)
    for i in range(QUARTERS):
        rows = slice(i * own_rows, (i + 1) * own_rows)
        cbuf[t, i] = jnp.concatenate([acc_k[rows, :] * SCALE, acc_v[rows, :]], 1).astype(BF16)
    dbuf[t, lo] = cbuf[t, lo]
    for j in range(1, QUARTERS):
        quarter_to(t, j).start()
    grk_ref[...] = (acc_k[plen:, :] * SCALE).astype(BF16)
    grv_ref[...] = acc_v[plen:, :].astype(BF16)

    @pl.when(t >= 1)
    def _():
        reduce_group(t - 1)

    @pl.when(t >= 2)
    def _():
        reduce_planes(t - 2)

    @pl.when(t == KV_HEADS - 1)
    def _():
        reduce_group(KV_HEADS - 1)
        reduce_planes(KV_HEADS - 2)
        reduce_planes(KV_HEADS - 1)

        @pl.loop(0, KV_HEADS)
        def _(h):
            for j in range(1, planes):
                planes_of(h, j).wait_send()
                term_to(h, j).wait_send()
            rows_of(h).wait_send()
            for r in range(2):
                cores_of(h, r).wait_send()
            for j in range(1, QUARTERS):
                quarter_to(h, j).wait_send()


def shards(
    query, resp_key, resp_value, prompt_key, prompt_value, grad_out, resp_lengths, resp_prompt
):
    rows = query.shape[0]
    own_rows = prompt_key.shape[0]
    plen = QUARTERS * own_rows
    width = KV_HEADS * D_HEAD
    planes = lax.axis_size("dp") // QUARTERS
    wide = pl.BlockSpec((rows, GROUP * D_HEAD), lambda h: (0, h))
    own = pl.BlockSpec((rows, D_HEAD), lambda h: (0, h))
    whole = pl.BlockSpec((own_rows, width), lambda h: (0, 0))
    smem = pl.BlockSpec(memory_space=pltpu.SMEM)
    sds = jax.ShapeDtypeStruct
    pair = (own_rows, 2 * D_HEAD)
    dma = pltpu.SemaphoreType.DMA
    return pl.pallas_call(
        kernel,
        grid=(KV_HEADS,),
        in_specs=[smem, smem, wide, wide, whole, whole, own, own],
        out_specs=[wide, own, own, whole, whole],
        scratch_shapes=[
            pltpu.VMEM((rows, rows), F32),
            pltpu.VMEM((plen + rows, D_HEAD), F32),
            pltpu.VMEM((plen + rows, D_HEAD), F32),
            pltpu.VMEM((KV_HEADS, 2, 2, planes) + pair, BF16),
            pltpu.VMEM((KV_HEADS, QUARTERS) + pair, BF16),
            pltpu.VMEM((KV_HEADS, QUARTERS) + pair, BF16),
            pltpu.VMEM((KV_HEADS, planes) + pair, BF16),
            pltpu.VMEM((KV_HEADS, planes) + pair, BF16),
            pltpu.VMEM((QUARTERS, 8, 128), F32),
            dma((KV_HEADS, planes - 1)),
            dma((KV_HEADS, planes - 1)),
            dma((KV_HEADS,)),
            dma((KV_HEADS,)),
            dma((KV_HEADS, 2)),
            dma((KV_HEADS, 2)),
            dma((KV_HEADS, QUARTERS - 1)),
            dma((KV_HEADS, QUARTERS - 1)),
            dma((KV_HEADS, planes - 1)),
            dma((KV_HEADS, planes - 1)),
            dma((QUARTERS - 1,)),
            dma((QUARTERS - 1,)),
        ],
        out_shape=[
            sds((rows, HEADS * D_HEAD), BF16),
            sds((rows, width), BF16),
            sds((rows, width), BF16),
            sds((own_rows, width), BF16),
            sds((own_rows, width), BF16),
        ],
        compiler_params=pltpu.CompilerParams(
            dimension_semantics=("arbitrary",), vmem_limit_bytes=61 * 1024 * 1024,
            collective_id=0, has_side_effects=True,
        ),
    )(resp_prompt, resp_lengths, query, grad_out, prompt_key, prompt_value, resp_key, resp_value)


def solution(mesh):
    rows = P(("groups", "dp"), None)
    return jax.shard_map(
        shards,
        mesh=mesh,
        in_specs=(rows,) * 7 + (P(("groups", "dp")),),
        out_specs=(rows,) * 5,
        check_vma=False,
    )
```
